32 devices in a mesh: dp: 16 (over z, y, core), ctx: 2 (over x).
Axes of the slice: x: 2, y: 2, z: 4, core: 2. Of those that a mesh axis runs over, the one named last changes fastest.
Arguments:
- frames: bfloat16 [16, 1024, 1280], P('dp', 'ctx'), may hold values from -6 to 6
- conv_taps: float32 [31, 1280], replicated, may hold values from -1 to 1
- conv_gain: float32 [1280], replicated, may hold values from 0.1 to 1.9
- w_kv: bfloat16 [1280, 2560], P('dp'), may hold values from -0.15625 to 0.15625
- queries: bfloat16 [16, 32, 1280], P('dp', 'ctx'), may hold values from -6 to 6
- out_grad: bfloat16 [16, 32, 1280], P('dp', 'ctx'), may hold values from -6 to 6
- frame_len: int32 [16], P('dp'), may hold values from 256 to 1024
- token_len: int32 [16], P('dp'), may hold values from 8 to 32
Outputs:
- frames_grad: bfloat16 [16, 1024, 1280], P('dp', 'ctx')
- taps_grad: float32 [31, 1280], replicated
- gain_grad: float32 [1280], replicated
- w_kv_grad: float32 [1280, 2560], P('dp')
- queries_grad: bfloat16 [16, 32, 1280], P('dp', 'ctx')
The draws below stay inside these ranges and needn't reach their ends.
Inputs may be any that keep to these rules, and one draw needn't show every extreme that they name: frames at positions of frame_len[b] or beyond are padding of utterance b. Tokens at positions of token_len[b] or beyond are padding of utterance b.
All inputs are finite; a program needn't handle non-finite values.
Results may differ from the reference program's by a relative error of at most 0.012.
Values may be sent and summed in bfloat16 or wider, within the bound.
A program may use at most 128 MiB of HBM per device.

```python
import jax
import jax.numpy as jnp
from jax import lax

D = 1280
HEADS = 20
KSIZE = 31
UTTS = 16
FRAMES = 1024
TOKQ = 32


def place_ends(array, key, least, top_value):
    dims = array.shape
    index_at = [jax.random.randint(jax.random.fold_in(key, axis), (), 0, dims[axis]) for axis in range(len(dims))]
    array = array.at[tuple(index_at)].set(least)
    longest = dims.index(max(dims))
    index_at[longest] = (index_at[longest] + 1) % dims[longest]
    return array.at[tuple(index_at)].set(top_value)


def steps_of(stream_key, extent, pieces, smallest, largest):
    level, own = 1.0, jax.random.fold_in(stream_key, 6)
    for dim, parts in pieces:
        draws = jnp.exp(jax.random.uniform(jax.random.fold_in(own, dim), (parts,), jnp.float32, smallest / len(pieces), largest / len(pieces)))
        level = level * jnp.repeat(draws, extent[dim] // parts).reshape([-1 if axis == dim else 1 for axis in range(len(extent))])
    return level


def bell_draw(rng, shape, scale, limit, cuts=(), kind=jnp.bfloat16):
    drawn = scale * jax.random.normal(rng, shape, jnp.float32)
    if cuts:
        drawn = drawn * steps_of(rng, shape, cuts, -0.22, 0.18)
    return jnp.clip(drawn, -limit, limit).astype(kind)


def setup_inputs(seed: int = 0) -> dict:
    streams_of = jax.random.split(jax.random.key(seed), 9)
    frames = bell_draw(streams_of[0], (UTTS, FRAMES, D), 1.0, 6.0, ((0, 16), (1, 2)))
    conv_taps = bell_draw(streams_of[1], (KSIZE, D), KSIZE ** -0.5, 1.0, (), jnp.float32)
    conv_gain = jnp.clip(1.0 + 0.18 * jax.random.normal(streams_of[2], (D,), jnp.float32), 0.1, 1.9)
    w_kv = bell_draw(streams_of[3], (D, 2 * D), D ** -0.5, 0.15625, ((0, 16),))
    queries = bell_draw(streams_of[4], (UTTS, TOKQ, D), 1.0, 6.0, ((0, 16), (1, 2)))
    out_grad = bell_draw(streams_of[5], (UTTS, TOKQ, D), 1.0, 6.0, ((0, 16), (1, 2)))
    frame_len = place_ends(jax.random.randint(streams_of[6], (UTTS,), FRAMES // 4, FRAMES + 1), jax.random.fold_in(streams_of[6], 1), FRAMES // 4, FRAMES).astype(jnp.int32)
    token_len = place_ends(jax.random.randint(streams_of[7], (UTTS,), TOKQ // 4, TOKQ + 1), jax.random.fold_in(streams_of[7], 1), TOKQ // 4, TOKQ).astype(jnp.int32)
    return {"frames": frames, "conv_taps": conv_taps, "conv_gain": conv_gain, "w_kv": w_kv, "queries": queries, "out_grad": out_grad, "frame_len": frame_len, "token_len": token_len}


def rounded(values):
    return lax.optimization_barrier(values.astype(jnp.bfloat16)).astype(jnp.float32)


def conv_time(padded, conv_taps, length):
    total = jnp.zeros((length, padded.shape[1]), jnp.float32)
    for tap_idx in range(conv_taps.shape[0]):
        total = total + conv_taps[tap_idx] * padded[tap_idx:tap_idx + length].astype(jnp.float32)
    return total


def silu_slope(gated):
    sigma = jax.nn.sigmoid(gated)
    return sigma * (1.0 + gated * (1.0 - sigma))


def reference(frames, conv_taps, conv_gain, w_kv, queries, out_grad, frame_len, token_len):
    model_width = frames.shape[2]
    head_count = HEADS
    head_dim = model_width // head_count
    scale = head_dim ** -0.5
    tap_count = conv_taps.shape[0]
    rim_width = tap_count // 2

    def utterance(carried, inputs):
        frame_rows, query_rows, grad_rows, live_frames, live_tokens = inputs
        length = frame_rows.shape[0]
        tokens = query_rows.shape[0]
        zero_rim = jnp.zeros((rim_width, model_width), frame_rows.dtype)
        padded = jnp.concatenate([zero_rim, frame_rows, zero_rim], 0)
        conv_out = conv_time(padded, conv_taps, length)
        gated = conv_gain * conv_out
        encoded = (frame_rows.astype(jnp.float32) + jax.nn.silu(gated)).astype(jnp.bfloat16)
        key_values = jnp.dot(encoded, w_kv, preferred_element_type=jnp.float32).astype(jnp.bfloat16)
        live_mask = (jnp.arange(length) < live_frames).astype(jnp.float32)
        token_mask = (jnp.arange(tokens) < live_tokens).astype(jnp.bfloat16)
        grad_block = grad_rows * token_mask[:, None]
        q_heads = query_rows.astype(jnp.float32).reshape(tokens, head_count, head_dim)
        k_heads = key_values[:, :model_width].astype(jnp.float32).reshape(length, head_count, head_dim)
        v_heads = key_values[:, model_width:].astype(jnp.float32).reshape(length, head_count, head_dim)
        g_heads = grad_block.astype(jnp.float32).reshape(tokens, head_count, head_dim)
        exp_scores = jnp.exp(jnp.einsum("thd,fhd->htf", q_heads, k_heads) * scale) * live_mask
        totals = jnp.sum(exp_scores, axis=2)
        weighted = jnp.einsum("htf,fhd->thd", rounded(exp_scores), v_heads)
        attended = weighted / totals.T[:, :, None]
        delta_rows = jnp.sum(g_heads * attended, axis=2)
        attn_prob = exp_scores / totals[:, :, None]
        d_prob = jnp.einsum("thd,fhd->htf", g_heads, v_heads)
        d_score = rounded(attn_prob * (d_prob - delta_rows.T[:, :, None]))
        query_grad = jnp.einsum("htf,fhd->thd", d_score, k_heads) * scale
        query_grad = query_grad.reshape(tokens, model_width).astype(jnp.bfloat16)
        key_grad = (jnp.einsum("htf,thd->fhd", d_score, q_heads) * scale).reshape(length, model_width)
        value_grad = jnp.einsum("htf,thd->fhd", rounded(attn_prob), g_heads).reshape(length, model_width)
        kv_grad = jnp.concatenate([key_grad, value_grad], 1).astype(jnp.bfloat16)
        w_term = lax.dot_general(encoded, kv_grad, (((0,), (0,)), ((), ())), preferred_element_type=jnp.float32)
        enc_grad = lax.dot_general(kv_grad, w_kv, (((1,), (1,)), ((), ())), preferred_element_type=jnp.float32)
        gated_grad = enc_grad * silu_slope(gated)
        gain_term = jnp.sum(gated_grad * conv_out, axis=0)
        conv_grad = gated_grad * conv_gain
        tap_terms = jnp.stack([jnp.sum(conv_grad * padded[tap_idx:tap_idx + length].astype(jnp.float32), axis=0) for tap_idx in range(tap_count)])
        zero_grad = jnp.zeros((rim_width, model_width), jnp.float32)
        padded_grad = jnp.concatenate([zero_grad, conv_grad, zero_grad], 0)
        back_sum = jnp.zeros((length, model_width), jnp.float32)
        for tap_idx in range(tap_count):
            offset = 2 * rim_width - tap_idx
            back_sum = back_sum + conv_taps[tap_idx] * padded_grad[offset:offset + length]
        frame_grad = (enc_grad + back_sum).astype(jnp.bfloat16)
        w_sum, tap_sum, gain_sum = carried
        return (w_sum + w_term, tap_sum + tap_terms, gain_sum + gain_term), (frame_grad, query_grad)

    start_sums = (jnp.zeros((model_width, 2 * model_width), jnp.float32), jnp.zeros((tap_count, model_width), jnp.float32), jnp.zeros((model_width,), jnp.float32))
    sums, grads = lax.scan(utterance, start_sums, (frames, queries, out_grad, frame_len, token_len))
    return grads[0], sums[1], sums[2], sums[0], grads[1]
```

```python
import functools

import jax
import jax.numpy as jnp
from jax import lax
from jax.experimental import pallas as pl
from jax.experimental.pallas import tpu as pltpu
from jax.sharding import PartitionSpec as P

HEADS = 20
PACK = 4
LANES = 128
VMEM_BYTES = 48 * 1024 * 1024
F32 = jnp.float32
BF16 = jnp.bfloat16


def shifted(value, axis, steps):
    count = lax.axis_size(axis)
    pairs = [(source, (source + steps) % count) for source in range(count)]
    return lax.ppermute(value, axis, pairs)


def rims(block, width):
    count = lax.axis_size("ctx")
    forward = [(i, i + 1) for i in range(count - 1)]
    backward = [(i + 1, i) for i in range(count - 1)]
    low = lax.ppermute(block[block.shape[0] - width :], "ctx", forward)
    high = lax.ppermute(block[:width], "ctx", backward)
    return low, high


def gather_tokens(block):
    parts = [block]
    for step in range(1, lax.axis_size("ctx")):
        parts.append(shifted(block, "ctx", step))
    return jnp.concatenate(parts, axis=0)


def sum_ctx(value):
    total = value
    for step in range(1, lax.axis_size("ctx")):
        total = total + shifted(value, "ctx", step)
    return total


def sum_all(value):
    for axis in ("dp", "ctx"):
        count = lax.axis_size(axis)
        if count & (count - 1):
            value = lax.psum(value, axis)
            continue
        step = 1
        while step < count:
            value = value + lax.ppermute(value, axis, [(i, i ^ step) for i in range(count)])
            step *= 2
    return value


def conv_time(padded, conv_taps, length):
    total = jnp.zeros((length, padded.shape[1]), F32)
    for tap_idx in range(conv_taps.shape[0]):
        total = total + conv_taps[tap_idx] * padded[tap_idx : tap_idx + length].astype(F32)
    return total


def packed(block, scale):
    tokens, width = block.shape
    groups = HEADS // PACK
    cols = width // groups
    head_dim = cols // PACK
    rows = block.reshape(tokens, groups, cols).transpose(1, 0, 2)[:, None]
    own = (jnp.arange(cols)[None] // head_dim == jnp.arange(PACK)[:, None]).astype(F32) * scale
    return (rows.astype(F32) * own[None, :, None, :]).astype(BF16).reshape(groups, PACK * tokens, cols)


def score_kernel(limit_ref, kv_ref, q_ref, g_ref, e_ref, d_ref, s_ref):
    groups, lanes, cols = q_ref.shape
    length = kv_ref.shape[0]
    width = groups * cols
    live = lax.broadcasted_iota(jnp.int32, (length, lanes), 0) < limit_ref[0]
    dims = (((1,), (1,)), ((), ()))
    s_ref[...] = jnp.zeros_like(s_ref)
    for j in range(groups):
        keys = kv_ref[:, j * cols : (j + 1) * cols]
        values = kv_ref[:, width + j * cols : width + (j + 1) * cols]
        scores = lax.dot_general(keys, q_ref[j], dims, preferred_element_type=F32)
        exps = jnp.where(live, jnp.exp(scores), 0.0)
        dprob = lax.dot_general(values, g_ref[j], dims, preferred_element_type=F32)
        e_ref[:, j * lanes : (j + 1) * lanes] = exps
        d_ref[:, j * lanes : (j + 1) * lanes] = dprob
        s_ref[j : j + 1] = jnp.sum(exps, axis=0, keepdims=True)
        s_ref[8 + j : 9 + j] = jnp.sum(exps.astype(BF16).astype(F32) * dprob, axis=0, keepdims=True)


def grad_kernel(e_ref, d_ref, s_ref, kv_ref, q_ref, g_ref, kvg_ref, qg_ref):
    groups, lanes, cols = q_ref.shape
    width = groups * cols
    tokens = lanes // PACK
    head_dim = cols // PACK
    head_of = lax.broadcasted_iota(jnp.int32, (tokens, cols), 1) // head_dim
    for j in range(groups):
        inverse = 1.0 / s_ref[j : j + 1]
        delta = s_ref[8 + j : 9 + j] * inverse
        prob = e_ref[:, j * lanes : (j + 1) * lanes] * inverse
        dscore = (prob * (d_ref[:, j * lanes : (j + 1) * lanes] - delta)).astype(BF16)
        kvg_ref[:, j * cols : (j + 1) * cols] = jnp.dot(
            dscore, q_ref[j], preferred_element_type=F32
        ).astype(BF16)
        kvg_ref[:, width + j * cols : width + (j + 1) * cols] = jnp.dot(
            prob.astype(BF16), g_ref[j], preferred_element_type=F32
        ).astype(BF16)
        full = lax.dot_general(
            dscore,
            kv_ref[:, j * cols : (j + 1) * cols],
            (((0,), (0,)), ((), ())),
            preferred_element_type=F32,
        )
        total = jnp.zeros((tokens, cols), F32)
        for h in range(PACK):
            total = total + jnp.where(head_of == h, full[h * tokens : (h + 1) * tokens], 0.0)
        qg_ref[:, j * cols : (j + 1) * cols] = total


def taps_kernel(tap_count, g_ref, x_ref, t_ref):
    length = g_ref.shape[0]

    def step(i, sums):
        base = pl.multiple_of(i * 8, 8)
        grad = g_ref[pl.ds(base, 8), :]
        return tuple(sums[k] + grad * x_ref[pl.ds(base + k, 8), :] for k in range(tap_count))

    zero = jnp.zeros((8, g_ref.shape[1]), F32)
    sums = lax.fori_loop(0, length // 8, step, (zero,) * tap_count)
    t_ref[...] = jnp.zeros_like(t_ref)
    for k in range(tap_count):
        t_ref[k : k + 1, :] = jnp.sum(sums[k], axis=0, keepdims=True)


def back_kernel(tap_count, taps_ref, g_ref, e_ref, o_ref):
    rows = 64

    def step(i, carry):
        base = pl.multiple_of(i * rows, rows)
        total = e_ref[pl.ds(base, rows), :]
        for k in range(tap_count):
            total = total + taps_ref[k : k + 1, :] * g_ref[pl.ds(base + tap_count - 1 - k, rows), :]
        o_ref[pl.ds(base, rows), :] = total.astype(BF16)
        return carry

    lax.fori_loop(0, e_ref.shape[0] // rows, step, 0)


def whole_spec():
    return pl.BlockSpec(memory_space=pltpu.VMEM)


def column_spec(rows):
    return pl.BlockSpec((rows, LANES), lambda j: (0, j))


def per_device(frames, conv_taps, conv_gain, w_kv, queries, out_grad, frame_len, token_len):
    cycle_pos = lax.axis_index("ctx")
    length = frames.shape[1]
    width = frames.shape[2]
    tokens = queries.shape[1]
    tap_count = conv_taps.shape[0]
    rim = tap_count // 2
    scale = (width // HEADS) ** (-0.5)
    params = pltpu.CompilerParams(vmem_limit_bytes=VMEM_BYTES)

    w_full = lax.all_gather(w_kv, "dp", axis=0, tiled=True)
    block = frames[0]
    low, high = rims(block, rim)
    tail = -(length + 2 * rim) % 16
    padded = jnp.concatenate([low, block, high, jnp.zeros((tail, width), BF16)], axis=0).astype(F32)
    conv_out = conv_time(padded, conv_taps, length)
    gated = conv_gain * conv_out
    sigma = jax.nn.sigmoid(gated)
    encoded = (block.astype(F32) + gated * sigma).astype(BF16)
    slope = sigma * (1.0 + gated * (1.0 - sigma))

    token_pos = cycle_pos * tokens + jnp.arange(tokens)
    grad_block = out_grad[0] * (token_pos < token_len[0]).astype(BF16)[:, None]
    q_pack = packed(gather_tokens(queries[0]), scale)
    g_pack = packed(gather_tokens(grad_block), 1.0)
    groups, lanes, _ = q_pack.shape
    all_tokens = lanes // PACK
    limit = (frame_len - cycle_pos * length).astype(jnp.int32)

    key_values = jnp.dot(encoded, w_full, preferred_element_type=F32).astype(BF16)
    exps, dprob, stats = pl.pallas_call(
        score_kernel,
        out_shape=(
            jax.ShapeDtypeStruct((length, groups * lanes), F32),
            jax.ShapeDtypeStruct((length, groups * lanes), F32),
            jax.ShapeDtypeStruct((16, lanes), F32),
        ),
        in_specs=[pl.BlockSpec(memory_space=pltpu.SMEM)] + [whole_spec()] * 3,
        out_specs=(whole_spec(),) * 3,
        compiler_params=params,
    )(limit, key_values, q_pack, g_pack)
    count = lax.axis_size("ctx")
    parts = stats.reshape(16, PACK, count, tokens)
    total_parts = parts
    for step in range(1, count):
        total_parts = total_parts + jnp.roll(shifted(parts, "ctx", step), step, axis=2)
    stats = total_parts.reshape(16, lanes)
    kv_grad, q_part = pl.pallas_call(
        grad_kernel,
        out_shape=(
            jax.ShapeDtypeStruct((length, 2 * width), BF16),
            jax.ShapeDtypeStruct((all_tokens, width), F32),
        ),
        in_specs=[whole_spec()] * 6,
        out_specs=(whole_spec(),) * 2,
        compiler_params=params,
    )(exps, dprob, stats, key_values, q_pack, g_pack)

    w_part = lax.dot_general(
        encoded, kv_grad, (((0,), (0,)), ((), ())), preferred_element_type=F32
    ).astype(BF16)
    w_rows = lax.psum_scatter(w_part, "dp", scatter_dimension=0, tiled=True)

    q_parts = q_part.reshape(count, tokens, width)
    q_sum = q_parts[0]
    for step in range(1, count):
        q_sum = q_sum + shifted(q_parts[step], "ctx", -step)
    queries_grad = (q_sum * scale).astype(BF16)[None]

    enc_grad = lax.dot_general(
        kv_grad, w_full, (((1,), (1,)), ((), ())), preferred_element_type=F32
    )
    gated_grad = enc_grad * slope
    grad_low, grad_high = rims(gated_grad, rim)
    tap_rows = -(-tap_count // 8) * 8
    tap_sums = pl.pallas_call(
        functools.partial(taps_kernel, tap_count),
        grid=(width // LANES,),
        out_shape=jax.ShapeDtypeStruct((tap_rows, width), F32),
        in_specs=[column_spec(length), column_spec(padded.shape[0])],
        out_specs=column_spec(tap_rows),
        compiler_params=params,
    )(gated_grad, padded)
    tap_sums = sum_all(tap_sums)[:tap_count]
    taps_grad = tap_sums * conv_gain
    gain_grad = jnp.sum(tap_sums * conv_taps, axis=0)

    padded_grad = jnp.concatenate(
        [grad_low, gated_grad, grad_high, jnp.zeros((tail, width), F32)], axis=0
    )
    scaled_taps = jnp.concatenate(
        [conv_taps * conv_gain, jnp.zeros((tap_rows - tap_count, width), F32)], axis=0
    )
    frames_grad = pl.pallas_call(
        functools.partial(back_kernel, tap_count),
        grid=(width // LANES,),
        out_shape=jax.ShapeDtypeStruct((length, width), BF16),
        in_specs=[column_spec(tap_rows), column_spec(padded_grad.shape[0]), column_spec(length)],
        out_specs=column_spec(length),
        compiler_params=params,
    )(scaled_taps, padded_grad, enc_grad)[None]

    if count == 2:
        w_kv_grad = w_rows.astype(F32) + shifted(w_rows, "ctx", 1).astype(F32)
    else:
        w_kv_grad = lax.psum(w_rows.astype(F32), "ctx")
    return (frames_grad, taps_grad, gain_grad, w_kv_grad, queries_grad)


def solution(mesh):
    placed = (
        P("dp", "ctx", None),
        P(),
        P(),
        P("dp", None),
        P("dp", "ctx", None),
        P("dp", "ctx", None),
        P("dp"),
        P("dp"),
    )
    return jax.shard_map(
        per_device,
        mesh=mesh,
        in_specs=placed,
        out_specs=(P("dp", "ctx", None), P(), P(), P("dp", None), P("dp", "ctx", None)),
        check_vma=False,
    )
```

```python
import functools

import jax
import jax.numpy as jnp
from jax import lax
from jax.experimental import pallas as pl
from jax.experimental.pallas import tpu as pltpu
from jax.sharding import PartitionSpec as P

HEADS = 20
PACK = 4
LANES = 128
VMEM_BYTES = 48 * 1024 * 1024
GATHER_GROUPS = (("offload", 0, 10),)
SCATTER_GROUPS = (("ctx", 0, 5), ("dp", 5, 10))
F32 = jnp.float32
BF16 = jnp.bfloat16


def shifted(value, axis, steps):
    count = lax.axis_size(axis)
    pairs = [(source, (source + steps) % count) for source in range(count)]
    return lax.ppermute(value, axis, pairs)


def rims(block, width):
    count = lax.axis_size("ctx")
    if count == 2:
        first = lax.axis_index("ctx") == 0
        other = exchange(
            jnp.where(first, block[block.shape[0] - width :], block[:width]), "ctx", 0
        )
        zero = jnp.zeros_like(other)
        return jnp.where(first, zero, other), jnp.where(first, other, zero)
    forward = [(i, i + 1) for i in range(count - 1)]
    backward = [(i + 1, i) for i in range(count - 1)]
    low = lax.ppermute(block[block.shape[0] - width :], "ctx", forward)
    high = lax.ppermute(block[:width], "ctx", backward)
    return low, high


def gather_tokens(block):
    parts = [block]
    for step in range(1, lax.axis_size("ctx")):
        parts.append(shifted(block, "ctx", step))
    return jnp.concatenate(parts, axis=0)


def sum_ctx(value):
    total = value
    for step in range(1, lax.axis_size("ctx")):
        total = total + shifted(value, "ctx", step)
    return total


def sum_all(value):
    for axis in ("dp", "ctx"):
        count = lax.axis_size(axis)
        if count & (count - 1):
            value = lax.psum(value, axis)
            continue
        step = 1
        while step < count:
            value = value + lax.ppermute(value, axis, [(i, i ^ step) for i in range(count)])
            step *= 2
    return value


def bits_of(axis):
    count = lax.axis_size(axis)
    return count.bit_length() - 1


def stages(path):
    dp = [("dp", bit) for bit in range(bits_of("dp"))]
    ctx = [("ctx", bit) for bit in range(bits_of("ctx"))]
    first = dp[:1] if path == "ctx" else dp[:2]
    return first + ctx + dp[len(first) :]


def exchange(value, axis, bit):
    count = lax.axis_size(axis)
    return lax.ppermute(value, axis, [(i, i ^ (1 << bit)) for i in range(count)])


def bit_at(axis, bit):
    return (lax.axis_index(axis) >> bit) & 1


def plain_sizes():
    return all(lax.axis_size(a) == 1 << bits_of(a) for a in ("dp", "ctx"))


def half_dim(value, axis, bit, open_bits):
    if axis == "ctx":
        return value.ndim - 1
    return len(open_bits) - 1 - sorted(open_bits).index(bit)


def scatter_sum(value, path):
    if path == "offload" or not plain_sizes():
        part = lax.psum_scatter(value, "dp", scatter_dimension=0, tiled=True)
        if lax.axis_size("ctx") == 2:
            return part.astype(F32) + shifted(part, "ctx", 1).astype(F32), []
        return lax.psum(part.astype(F32), "ctx"), []
    sums = []
    open_bits = list(range(bits_of("dp")))
    rows, cols = value.shape
    value = value.reshape([2] * len(open_bits) + [rows // lax.axis_size("dp"), cols])
    for axis, bit in stages(path):
        dim = half_dim(value, axis, bit, open_bits)
        half = value.shape[dim] // 2
        mine = bit_at(axis, bit)
        keep = lax.dynamic_slice_in_dim(value, mine * half, half, dim)
        send = lax.dynamic_slice_in_dim(value, (1 - mine) * half, half, dim)
        if axis == "dp":
            keep, send = jnp.squeeze(keep, dim), jnp.squeeze(send, dim)
            open_bits.remove(bit)
        value = (keep.astype(F32) + exchange(send, axis, bit).astype(F32)).astype(BF16)
        sums.append(value)
    for bit in reversed(range(bits_of("ctx"))):
        other = exchange(value, "ctx", bit)
        value = jnp.where(
            bit_at("ctx", bit) == 0,
            jnp.concatenate([value, other], axis=1),
            jnp.concatenate([other, value], axis=1),
        )
    return value.astype(F32), sums


def gather_rows(value, path):
    if path == "offload" or not plain_sizes():
        return lax.all_gather(value, "dp", axis=0, tiled=True)
    rows, cols = value.shape
    for bit in range(bits_of("ctx")):
        half = value.shape[1] // 2
        value = lax.dynamic_slice_in_dim(value, bit_at("ctx", bit) * half, half, 1)
    open_bits = []
    for axis, bit in reversed(stages(path)):
        other = exchange(value, axis, bit)
        if axis == "dp":
            open_bits.append(bit)
            dim = half_dim(value, axis, bit, open_bits)
            value, other = jnp.expand_dims(value, dim), jnp.expand_dims(other, dim)
        else:
            dim = value.ndim - 1
        value = jnp.where(
            bit_at(axis, bit) == 0,
            jnp.concatenate([value, other], axis=dim),
            jnp.concatenate([other, value], axis=dim),
        )
    return value.reshape(-1, cols)


def conv_time(padded, conv_taps, length):
    total = jnp.zeros((length, padded.shape[1]), F32)
    for tap_idx in range(conv_taps.shape[0]):
        total = total + conv_taps[tap_idx] * padded[tap_idx : tap_idx + length].astype(F32)
    return total


def packed(block, scale):
    tokens, width = block.shape
    groups = HEADS // PACK
    cols = width // groups
    head_dim = cols // PACK
    rows = block.reshape(tokens, groups, cols).transpose(1, 0, 2)[:, None]
    own = (jnp.arange(cols)[None] // head_dim == jnp.arange(PACK)[:, None]).astype(F32) * scale
    return (rows.astype(F32) * own[None, :, None, :]).astype(BF16).reshape(groups, PACK * tokens, cols)


def scores_of(limit_ref, kv_ref, q_ref, g_ref, j):
    groups, lanes, cols = q_ref.shape
    length = kv_ref.shape[0]
    width = groups * cols
    live = lax.broadcasted_iota(jnp.int32, (length, lanes), 0) < limit_ref[0]
    dims = (((1,), (1,)), ((), ()))
    keys = kv_ref[:, j * cols : (j + 1) * cols]
    values = kv_ref[:, width + j * cols : width + (j + 1) * cols]
    scores = lax.dot_general(keys, q_ref[j], dims, preferred_element_type=F32)
    dprob = lax.dot_general(values, g_ref[j], dims, preferred_element_type=F32)
    return jnp.where(live, jnp.exp(scores), 0.0), dprob, keys


def score_kernel(limit_ref, kv_ref, q_ref, g_ref, s_ref):
    s_ref[...] = jnp.zeros_like(s_ref)
    for j in range(q_ref.shape[0]):
        exps, dprob, _ = scores_of(limit_ref, kv_ref, q_ref, g_ref, j)
        s_ref[j : j + 1] = jnp.sum(exps, axis=0, keepdims=True)
        s_ref[8 + j : 9 + j] = jnp.sum(exps.astype(BF16).astype(F32) * dprob, axis=0, keepdims=True)


def grad_kernel(limit_ref, s_ref, kv_ref, q_ref, g_ref, kvg_ref, qg_ref):
    groups, lanes, cols = q_ref.shape
    width = groups * cols
    tokens = lanes // PACK
    head_dim = cols // PACK
    head_of = lax.broadcasted_iota(jnp.int32, (tokens, cols), 1) // head_dim
    for j in range(groups):
        exps, dprob, keys = scores_of(limit_ref, kv_ref, q_ref, g_ref, j)
        inverse = 1.0 / s_ref[j : j + 1]
        delta = s_ref[8 + j : 9 + j] * inverse
        prob = exps * inverse
        dscore = (prob * (dprob - delta)).astype(BF16)
        kvg_ref[:, j * cols : (j + 1) * cols] = jnp.dot(
            dscore, q_ref[j], preferred_element_type=F32
        ).astype(BF16)
        kvg_ref[:, width + j * cols : width + (j + 1) * cols] = jnp.dot(
            prob.astype(BF16), g_ref[j], preferred_element_type=F32
        ).astype(BF16)
        full = lax.dot_general(dscore, keys, (((0,), (0,)), ((), ())), preferred_element_type=F32)
        total = jnp.zeros((tokens, cols), F32)
        for h in range(PACK):
            total = total + jnp.where(head_of == h, full[h * tokens : (h + 1) * tokens], 0.0)
        qg_ref[:, j * cols : (j + 1) * cols] = total


def taps_kernel(tap_count, g_ref, x_ref, *rest):
    t_ref = rest[-1]
    length = g_ref.shape[0]

    def step(i, sums):
        base = pl.multiple_of(i * 8, 8)
        grad = g_ref[pl.ds(base, 8), :]
        return tuple(sums[k] + grad * x_ref[pl.ds(base + k, 8), :] for k in range(tap_count))

    zero = jnp.zeros((8, g_ref.shape[1]), F32)
    sums = lax.fori_loop(0, length // 8, step, (zero,) * tap_count)
    t_ref[...] = jnp.zeros_like(t_ref)
    for k in range(tap_count):
        t_ref[k : k + 1, :] = jnp.sum(sums[k], axis=0, keepdims=True)


def back_kernel(tap_count, taps_ref, g_ref, e_ref, *rest):
    o_ref = rest[-1]
    rows = 64

    def step(i, carry):
        base = pl.multiple_of(i * rows, rows)
        total = e_ref[pl.ds(base, rows), :]
        for k in range(tap_count):
            total = total + taps_ref[k : k + 1, :] * g_ref[pl.ds(base + tap_count - 1 - k, rows), :]
        o_ref[pl.ds(base, rows), :] = total.astype(BF16)
        return carry

    lax.fori_loop(0, e_ref.shape[0] // rows, step, 0)


def whole_spec():
    return pl.BlockSpec(memory_space=pltpu.VMEM)


def any_spec():
    return pl.BlockSpec(memory_space=pl.ANY)


def column_spec(rows):
    return pl.BlockSpec((rows, LANES), lambda j: (0, j))


def per_device(frames, conv_taps, conv_gain, w_kv, queries, out_grad, frame_len, token_len):
    cycle_pos = lax.axis_index("ctx")
    length = frames.shape[1]
    width = frames.shape[2]
    tokens = queries.shape[1]
    tap_count = conv_taps.shape[0]
    rim = tap_count // 2
    scale = (width // HEADS) ** (-0.5)
    params = pltpu.CompilerParams(vmem_limit_bytes=VMEM_BYTES)

    tenth = 2 * width // 10
    w_groups = [
        gather_rows(w_kv[:, lo * tenth : hi * tenth], path) for path, lo, hi in GATHER_GROUPS
    ]
    w_full = jnp.concatenate(w_groups, axis=1)
    block = frames[0]
    low, high = rims(block, rim)
    tail = -(length + 2 * rim) % 16
    padded = jnp.concatenate([low, block, high, jnp.zeros((tail, width), BF16)], axis=0).astype(F32)
    conv_out = conv_time(padded, conv_taps, length)
    gated = conv_gain * conv_out
    sigma = jax.nn.sigmoid(gated)
    encoded = (block.astype(F32) + gated * sigma).astype(BF16)
    slope = sigma * (1.0 + gated * (1.0 - sigma))

    token_pos = cycle_pos * tokens + jnp.arange(tokens)
    grad_block = out_grad[0] * (token_pos < token_len[0]).astype(BF16)[:, None]
    q_pack = packed(gather_tokens(queries[0]), scale)
    g_pack = packed(gather_tokens(grad_block), 1.0)
    groups, lanes, _ = q_pack.shape
    all_tokens = lanes // PACK
    limit = (frame_len - cycle_pos * length).astype(jnp.int32)

    key_values = jnp.concatenate(
        [jnp.dot(encoded, w, preferred_element_type=F32).astype(BF16) for w in w_groups], axis=1
    )
    smem = pl.BlockSpec(memory_space=pltpu.SMEM)
    stats = pl.pallas_call(
        score_kernel,
        out_shape=jax.ShapeDtypeStruct((16, lanes), F32),
        in_specs=[smem] + [whole_spec()] * 3,
        out_specs=whole_spec(),
        compiler_params=params,
    )(limit, key_values, q_pack, g_pack)
    count = lax.axis_size("ctx")
    parts = stats.reshape(16, PACK, count, tokens)
    total_parts = parts
    for step in range(1, count):
        total_parts = total_parts + jnp.roll(shifted(parts, "ctx", step), step, axis=2)
    stats = total_parts.reshape(16, lanes)
    kv_grad, q_part = pl.pallas_call(
        grad_kernel,
        out_shape=(
            jax.ShapeDtypeStruct((length, 2 * width), BF16),
            jax.ShapeDtypeStruct((all_tokens, width), F32),
        ),
        in_specs=[smem] + [whole_spec()] * 4,
        out_specs=(whole_spec(),) * 2,
        compiler_params=params,
    )(limit, stats, key_values, q_pack, g_pack)

    w_grads, w_parts, early, late = [], [], [], []
    for path, lo, hi in SCATTER_GROUPS:
        w_part = lax.dot_general(
            encoded,
            kv_grad[:, lo * tenth : hi * tenth],
            (((0,), (0,)), ((), ())),
            preferred_element_type=F32,
        ).astype(BF16)
        w_parts.append(w_part)
        w_sum, sums = scatter_sum(w_part, path)
        w_grads.append(w_sum)
        early += sums[:1]
        late += sums[1:2]
    w_kv_grad = jnp.concatenate(w_grads, axis=1)

    q_parts = q_part.reshape(count, tokens, width)
    q_sum = q_parts[0]
    for step in range(1, count):
        q_sum = q_sum + shifted(q_parts[step], "ctx", -step)
    queries_grad = (q_sum * scale).astype(BF16)[None]

    kv_late = lax.optimization_barrier((kv_grad, *w_parts))[0]
    enc_grad = lax.dot_general(
        kv_late, w_full, (((1,), (1,)), ((), ())), preferred_element_type=F32
    )
    gated_grad = enc_grad * slope
    grad_low, grad_high = rims(gated_grad, rim)
    tap_rows = -(-tap_count // 8) * 8
    tap_sums = pl.pallas_call(
        functools.partial(taps_kernel, tap_count),
        grid=(width // LANES,),
        out_shape=jax.ShapeDtypeStruct((tap_rows, width), F32),
        in_specs=[column_spec(length), column_spec(padded.shape[0])] + [any_spec()] * len(early),
        out_specs=column_spec(tap_rows),
        compiler_params=params,
        cost_estimate=pl.CostEstimate(
            flops=2 * tap_count * length * width,
            bytes_accessed=4 * tap_count * length * width,
            transcendentals=0,
        ),
    )(gated_grad, padded, *early)
    tap_sums = sum_all(tap_sums)[:tap_count]
    taps_grad = tap_sums * conv_gain
    gain_grad = jnp.sum(tap_sums * conv_taps, axis=0)

    padded_grad = jnp.concatenate(
        [grad_low, gated_grad, grad_high, jnp.zeros((tail, width), F32)], axis=0
    )
    scaled_taps = jnp.concatenate(
        [conv_taps * conv_gain, jnp.zeros((tap_rows - tap_count, width), F32)], axis=0
    )
    frames_grad = pl.pallas_call(
        functools.partial(back_kernel, tap_count),
        grid=(width // LANES,),
        out_shape=jax.ShapeDtypeStruct((length, width), BF16),
        in_specs=[column_spec(tap_rows), column_spec(padded_grad.shape[0]), column_spec(length)]
        + [any_spec()] * len(late),
        out_specs=column_spec(length),
        compiler_params=params,
        cost_estimate=pl.CostEstimate(
            flops=2 * tap_count * length * width,
            bytes_accessed=4 * tap_count * length * width,
            transcendentals=0,
        ),
    )(scaled_taps, padded_grad, enc_grad, *late)[None]
    return (frames_grad, taps_grad, gain_grad, w_kv_grad, queries_grad)


def solution(mesh):
    placed = (
        P("dp", "ctx", None),
        P(),
        P(),
        P("dp", None),
        P("dp", "ctx", None),
        P("dp", "ctx", None),
        P("dp"),
        P("dp"),
    )
    return jax.shard_map(
        per_device,
        mesh=mesh,
        in_specs=placed,
        out_specs=(P("dp", "ctx", None), P(), P(), P("dp", None), P("dp", "ctx", None)),
        check_vma=False,
    )
```
